32 devices in a mesh: mode: 4 (over z), slab: 8 (over y, x, core).
Axes of the slice: x: 2, y: 2, z: 4, core: 2. Of those that a mesh axis runs over, the one named last changes fastest.
Arguments:
- modes: bfloat16 [48, 3, 16, 64, 128], P('mode', None, 'slab'), may hold values from -100 to 100
- volume: float32 [16, 64, 128], P(None, ('mode', 'slab')), may hold values from 0.5 to 24
Outputs:
- convective: float32 [2304, 48], P(('mode', 'slab'))
- dissipation: float32 [48, 48], replicated
The draws below stay inside these ranges and needn't reach their ends.
All inputs are finite; a program needn't handle non-finite values.
Results may differ from the reference program's by a relative error of at most 0.0043.
Values may be sent and summed in bfloat16 or wider, within the bound.
No kernel may reach another device: no remote copies, remote signals or barrier semaphores. Data moves between devices by JAX's collectives and lax.ppermute only.
A program may use at most 128 MiB of HBM per device.

```python
import math
import jax
import jax.numpy as jnp
from jax import lax

NM = 48
NZ = 128
NX = 16
NY = 64


def draw_modes(key, part):
    key_shared, key_mix, key_amp, key_noise = jax.random.split(key, 4)
    shared = jax.random.truncated_normal(key_shared, -4.0, 4.0, (4, 3, NX, NY, NZ), jnp.float32)
    mixing = 0.6 * jax.random.truncated_normal(key_mix, -2.0, 2.0, (NM, 4), jnp.float32)
    amplitude = jnp.exp(jax.random.uniform(key_amp, (NM,), jnp.float32, math.log(0.5), math.log(2.0)))

    def one_mode(mode_number):
        noise_key = jax.random.fold_in(key_noise, mode_number)
        noise_field = jax.random.truncated_normal(noise_key, -4.0, 4.0, (3, NX, NY, NZ), jnp.float32)
        mode_field = noise_field
        for shared_number in range(4):
            mode_field = mode_field + mixing[mode_number, shared_number] * shared[shared_number]
        return (amplitude[mode_number] * mode_field).astype(jnp.bfloat16)
    return lax.map(one_mode, jnp.arange(NM, dtype=jnp.int32))


def draw_volume(key, part):
    rows_ramp = jnp.exp(math.log(3.0) * jnp.arange(NY, dtype=jnp.float32) / (NY - 1))
    base = jnp.exp(jax.random.uniform(key, (NX, NY, NZ), jnp.float32, math.log(0.5), math.log(2.0)))
    return base * rows_ramp[None, :, None]


def setup_inputs(seed: int = 0) -> dict:
    key_of = jax.random.split(jax.random.key(seed), 3)
    modes = draw_modes(jax.random.fold_in(key_of[2], 71), 0)
    volume = draw_volume(jax.random.fold_in(key_of[2], 71), 0)
    return dict(modes=modes, volume=volume)


viscosity = 0.05

def stencil(padded, dim, length):
    shifted = [lax.slice_in_dim(padded, offset, offset + length, axis=dim).astype(jnp.float32) for offset in range(5)]
    return (shifted[0] - 8.0 * shifted[1] + 8.0 * shifted[3] - shifted[4]) / 12.0

def gradient_fields(centre, x_padded, y_padded):
    z_padded = jnp.concatenate([centre[..., -2:], centre, centre[..., :2]], axis=4)
    along_x = stencil(x_padded, 2, centre.shape[2])
    along_y = stencil(y_padded, 3, centre.shape[3])
    along_z = stencil(z_padded, 4, centre.shape[4])
    return jnp.stack([along_x, along_y, along_z], axis=2).astype(jnp.bfloat16)

def contract(values, grad_all, weights, limit):
    mode_count = values.shape[0]
    cell_count = weights.size
    block_size = math.gcd(cell_count, limit)
    flat_values = values.reshape(mode_count, 3, cell_count)
    flat_grads = grad_all.reshape(mode_count, 3, 3, cell_count)
    flat_weights = weights.reshape(cell_count)

    def one_step(number, running):
        first_cell = (number * block_size).astype(jnp.int32)
        piece_values = lax.dynamic_slice_in_dim(flat_values, first_cell, block_size, 2)
        piece_grads = lax.dynamic_slice_in_dim(flat_grads, first_cell, block_size, 3)
        piece_weights = lax.dynamic_slice_in_dim(flat_weights, first_cell, block_size, 0)
        values_wide = piece_values.astype(jnp.float32)
        grads_wide = piece_grads.astype(jnp.float32)
        carried = values_wide[:, None, None, 0, :] * grads_wide[None, :, :, 0, :]
        carried = carried + values_wide[:, None, None, 1, :] * grads_wide[None, :, :, 1, :]
        carried = carried + values_wide[:, None, None, 2, :] * grads_wide[None, :, :, 2, :]
        carried = (carried * piece_weights).astype(jnp.bfloat16).reshape(mode_count * mode_count, 3 * block_size)
        conv_add = lax.dot_general(piece_values.reshape(mode_count, 3 * block_size), carried, (((1,), (1,)), ((), ())), preferred_element_type=jnp.float32)
        weighted = (grads_wide * piece_weights).astype(jnp.bfloat16).reshape(mode_count, 9 * block_size)
        diss_add = lax.dot_general(piece_grads.reshape(mode_count, 9 * block_size), weighted, (((1,), (1,)), ((), ())), preferred_element_type=jnp.float32)
        return (running[0] + conv_add, running[1] + diss_add)
    start_conv = jnp.zeros((mode_count, mode_count * mode_count), jnp.float32)
    start_diss = jnp.zeros((mode_count, mode_count), jnp.float32)
    conv_sum, diss_sum = lax.fori_loop(0, cell_count // block_size, one_step, (start_conv, start_diss))
    return (conv_sum.reshape(mode_count * mode_count, mode_count), diss_sum)

def reference(modes, volume):
    row_block = math.gcd(NY, 8)
    block_total = NY // row_block
    cell_total = NX * NY * NZ

    def one_rows(running, row_number):
        first_row = (row_number * row_block).astype(jnp.int32)
        wanted = first_row - 2 + jnp.arange(row_block + 4, dtype=jnp.int32)
        inside = (wanted >= 0) & (wanted < NY)
        clipped = jnp.clip(wanted, 0, NY - 1).astype(jnp.int32)
        taken = jnp.take(modes, clipped, axis=3)
        y_padded = jnp.where(inside[None, None, None, :, None], taken, jnp.zeros((), modes.dtype))
        centre = y_padded[:, :, :, 2:-2]
        x_padded = jnp.pad(centre, ((0, 0), (0, 0), (2, 2), (0, 0), (0, 0)))
        grad_all = gradient_fields(centre, x_padded, y_padded)
        weights = lax.dynamic_slice_in_dim(volume, first_row, row_block, 1)
        conv_add, diss_add = contract(centre, grad_all, weights, 4096)
        return ((running[0] + conv_add, running[1] + diss_add), None)
    start = (jnp.zeros((NM * NM, NM), jnp.float32), jnp.zeros((NM, NM), jnp.float32))
    (conv_sum, diss_sum), unused = lax.scan(one_rows, start, jnp.arange(block_total, dtype=jnp.int32))
    convective = conv_sum * (1.0 / math.sqrt(cell_total))
    dissipation = diss_sum * (viscosity / cell_total)
    return (convective, dissipation)
```

```python
import functools
import math

import jax
import jax.numpy as jnp
from jax import lax
from jax.experimental import pallas as pl
from jax.experimental.pallas import tpu as pltpu
from jax.sharding import PartitionSpec as P

viscosity = 0.05
bf16 = jnp.bfloat16
f32 = jnp.float32
VMEM_LIMIT = 56 * 2**20
FIRST = 0.5

vmem = pl.BlockSpec(memory_space=pltpu.VMEM)
smem = pl.BlockSpec(memory_space=pltpu.SMEM)


def assemble_kernel(me_ref, *refs):
    blocks, out_ref, wide = refs[:-2], refs[-2], refs[-1]
    local = blocks[0].shape[1] // 6
    total = local * len(blocks)

    def one_row(row, unused):
        for shift, block in enumerate(blocks):
            owner = me_ref[0] ^ shift
            values = block[row].astype(f32)
            for part in range(6):
                for piece in range(wide.shape[0]):
                    wide[piece, pl.ds(part * total + owner * local, local), :] = values[
                        part * local : (part + 1) * local, piece * 128 : (piece + 1) * 128
                    ]
        for piece in range(wide.shape[0]):
            out_ref[row, :, piece * 128 : (piece + 1) * 128] = wide[piece].astype(bf16)
        return unused

    lax.fori_loop(0, out_ref.shape[0], one_row, 0)


def assemble(me, blocks):
    rows, height, lanes = blocks[0].shape
    return pl.pallas_call(
        assemble_kernel,
        in_specs=[smem] + [vmem] * len(blocks),
        out_specs=vmem,
        out_shape=jax.ShapeDtypeStruct((rows, height * len(blocks), lanes), bf16),
        scratch_shapes=[pltpu.VMEM((lanes // 128, height * len(blocks), 128), f32)],
        compiler_params=pltpu.CompilerParams(vmem_limit_bytes=VMEM_LIMIT),
        name="assemble",
    )(me, *blocks)


def central(first, second, fourth, fifth):
    return ((first - 8.0 * second + 8.0 * fourth - fifth) / 12.0).astype(bf16)


def galerkin_kernel(plan, has_sum, rows_y, *refs):
    runs, field_plan, halo_plan = plan
    count = len(halo_plan)
    stride = 3 if runs > 1 else 1
    refs = list(refs)
    conv_in, diss_in = (refs.pop(0), refs.pop(0)) if has_sum else (None, None)
    volume_ref = refs.pop(0)
    fields, low, high, slopes_ref, values, stationary, carried, volumes = refs[-8:]
    conv_ref, diss_ref = refs[-10:-8]
    sources = refs[:-10]
    for slot, (operand, row) in enumerate(field_plan):
        fields[slot] = sources[operand][row]
    for slot, (low_operand, high_operand, row, cell_row) in enumerate(halo_plan):
        low[slot] = sources[low_operand][row]
        high[slot] = sources[high_operand][row]
        volumes[slot] = volume_ref[cell_row]
    if has_sum:
        conv_ref[...] = conv_in[...]
        diss_ref[...] = diss_in[...]
    else:
        conv_ref[...] = jnp.zeros_like(conv_ref)
        diss_ref[...] = jnp.zeros_like(diss_ref)

    height, lanes = fields.shape[1:]
    half = height // 2
    mode_count = half // 3
    row_y = lax.broadcasted_iota(jnp.int32, (height, lanes), 1) % rows_y

    def shifted(array, step):
        moved = pltpu.roll(array, (-step) % lanes, 1)
        inside = (row_y + step >= 0) & (row_y + step < rows_y)
        return jnp.where(inside, moved, 0.0)

    def one_step(step, unused):
        base = step * stride
        before = fields[base].astype(f32)
        here = fields[base + 1].astype(f32)
        after = fields[base + 2].astype(f32)
        left = low[step].astype(f32)
        right = high[step].astype(f32)
        along_x = central(
            left,
            jnp.concatenate([left[:, rows_y:], here[:, : lanes - rows_y]], axis=1),
            jnp.concatenate([here[:, rows_y:], right[:, : lanes - rows_y]], axis=1),
            right,
        )
        along_y = central(shifted(here, -2), shifted(here, -1), shifted(here, 1), shifted(here, 2))
        along_z = jnp.concatenate(
            [
                central(before[:half], before[half:], here[half:], after[:half]),
                central(before[half:], here[:half], after[:half], after[half:]),
            ],
            axis=0,
        )
        weights = volumes[step]
        weighted = []
        for parity in range(2):
            span = pl.ds(parity * lanes, lanes)
            values[:, span] = fields[base + 1, parity * half : (parity + 1) * half, :]
            product = here[parity * half : (parity + 1) * half] * weights[parity : parity + 1]
            coarse = product.astype(bf16)
            fine = (product - coarse.astype(f32)).astype(bf16)
            for comp in range(3):
                rows = slice(comp * mode_count, (comp + 1) * mode_count)
                place = pl.ds((2 * comp + parity) * lanes, lanes)
                stationary[:mode_count, place] = coarse[rows]
                stationary[mode_count:, place] = fine[rows]
        for comp in range(3):
            for direction, along in enumerate((along_x, along_y, along_z)):
                pieces = [
                    along[parity * half + comp * mode_count : parity * half + (comp + 1) * mode_count]
                    for parity in range(2)
                ]
                number = comp * 3 + direction
                for parity in range(2):
                    slopes_ref[
                        number * mode_count : (number + 1) * mode_count,
                        parity * lanes : (parity + 1) * lanes,
                    ] = pieces[parity]
                    scaled = pieces[parity].astype(f32) * weights[parity : parity + 1]
                    weighted.append(scaled.astype(bf16))
        diss_ref[...] += sum(
            lax.dot_general(
                slopes_ref[number * mode_count : (number + 1) * mode_count, :],
                jnp.concatenate(weighted[2 * number : 2 * number + 2], axis=1),
                (((1,), (1,)), ((), ())),
                preferred_element_type=f32,
            )
            for number in range(9)
        )
        width = 2 * lanes
        for j in range(mode_count):
            rows = [
                jnp.broadcast_to(
                    values[b * mode_count + j : b * mode_count + j + 1, :], (mode_count, width)
                )
                for b in range(3)
            ]
            for a in range(3):
                slopes = [
                    slopes_ref[(a * 3 + b) * mode_count : (a * 3 + b + 1) * mode_count, :]
                    for b in range(3)
                ]
                total = rows[0] * slopes[0] + rows[1] * slopes[1] + rows[2] * slopes[2]
                carried[j * mode_count : (j + 1) * mode_count, a * width : (a + 1) * width] = total
        conv_ref[...] += lax.dot_general(
            carried[...], stationary[...], (((1,), (1,)), ((), ())), preferred_element_type=f32
        )
        return unused

    lax.fori_loop(0, count, one_step, 0)


def galerkin(sums, volume, sources, plan, rows_y):
    runs, field_plan, halo_plan = plan
    height, lanes = sources[0].shape[1:]
    mode_count = height // 6
    operands = list(sums or ()) + [volume] + list(sources)
    return pl.pallas_call(
        functools.partial(galerkin_kernel, plan, sums is not None, rows_y),
        in_specs=[vmem] * len(operands),
        out_specs=(vmem, vmem),
        out_shape=(
            jax.ShapeDtypeStruct((mode_count * mode_count, 2 * mode_count), f32),
            jax.ShapeDtypeStruct((mode_count, mode_count), f32),
        ),
        scratch_shapes=[
            pltpu.VMEM((len(field_plan), height, lanes), bf16),
            pltpu.VMEM((len(halo_plan), height, lanes), bf16),
            pltpu.VMEM((len(halo_plan), height, lanes), bf16),
            pltpu.VMEM((9 * mode_count, 2 * lanes), bf16),
            pltpu.VMEM((3 * mode_count, 2 * lanes), bf16),
            pltpu.VMEM((2 * mode_count, 6 * lanes), bf16),
            pltpu.VMEM((mode_count * mode_count, 6 * lanes), bf16),
            pltpu.VMEM((len(halo_plan), 2, lanes), f32),
        ],
        compiler_params=pltpu.CompilerParams(vmem_limit_bytes=VMEM_LIMIT),
        name="galerkin",
    )(*operands)


def local_volume(volume, planes, cells_z):
    slabs = lax.axis_size("slab")
    owners = lax.axis_size("mode")
    rows = volume.shape[1]
    split = volume.reshape(slabs, planes, rows, owners, cells_z).transpose(3, 0, 4, 1, 2)
    split = split.reshape(owners * slabs, cells_z * planes * rows)
    moved = lax.all_to_all(split, ("mode", "slab"), 0, 0, tiled=True)
    moved = moved.reshape(owners * slabs, cells_z, planes, rows).transpose(1, 2, 0, 3)
    return moved.reshape(cells_z // 2, 2, planes * owners * slabs * rows)


def per_device(modes, volume):
    local, comps, planes, rows_y, cells = modes.shape
    owners = lax.axis_size("mode")
    slabs = lax.axis_size("slab")
    devices = owners * slabs
    mode_count = local * owners
    lanes = planes * rows_y
    pairs = cells // 2 // owners
    me = lax.axis_index("mode")
    me_word = me.astype(jnp.int32).reshape(1)

    turned = modes.transpose(4, 1, 0, 2, 3).reshape(cells // 2, 2 * comps * local, lanes)
    first = int(pairs * FIRST)
    spans = ((0, first), (first, pairs))

    def row_of(target, row):
        return lax.rem(target * pairs + row + cells // 2, cells // 2)

    def take(target, chunk):
        if chunk < 2:
            start, stop = spans[chunk]
            return lax.dynamic_slice_in_dim(turned, target * pairs + start, stop - start, 0)
        return jnp.concatenate(
            [
                lax.dynamic_slice_in_dim(turned, row_of(target, row), 1, 0)
                for row in (-1, pairs)
            ],
            axis=0,
        )

    fields = []
    for chunk in range(3):
        blocks = [take(me, chunk)]
        for shift in range(1, owners):
            exchange = [(source, source ^ shift) for source in range(owners)]
            blocks.append(lax.ppermute(take(me ^ shift, chunk), "mode", exchange))
        fields.append(assemble(me_word, blocks))
    weights = local_volume(volume, planes, cells // owners)

    forward = [(source, source + 1) for source in range(slabs - 1)]
    backward = [(target, source) for source, target in forward]
    lows = [lax.ppermute(fields[chunk], "slab", forward) for chunk in range(2)]
    highs = [lax.ppermute(fields[chunk], "slab", backward) for chunk in range(2)]

    def place(row):
        if row < 0:
            return (2, 0)
        if row >= pairs:
            return (2, 1)
        return (0, row) if row < first else (1, row - first)

    def plan_of(runs):
        field_plan, halo_plan = [], []
        for start, stop in runs:
            field_plan += [place(row) for row in range(start - 1, stop + 1)]
            for row in range(start, stop):
                chunk, inner = place(row)
                halo_plan.append((3 + chunk, 5 + chunk, inner, row))
        return (len(runs), field_plan, halo_plan)

    def compact(plan, sources):
        runs, field_plan, halo_plan = plan
        used = sorted(
            {entry[0] for entry in field_plan}
            | {entry[0] for entry in halo_plan}
            | {entry[1] for entry in halo_plan}
        )
        number = {operand: place for place, operand in enumerate(used)}
        field_plan = tuple((number[operand], row) for operand, row in field_plan)
        halo_plan = tuple((number[p], number[q], row, cell) for p, q, row, cell in halo_plan)
        return [sources[operand] for operand in used], (runs, field_plan, halo_plan)

    sources = fields + lows + highs
    sums = None
    for runs in ([(1, first - 1)], [(first - 1, pairs - 1)], [(pairs - 1, pairs), (0, 1)]):
        chosen, plan = compact(plan_of(runs), sources)
        sums = galerkin(sums, weights, chosen, plan, rows_y)
    conv, diss = sums
    conv = conv[:, :mode_count] + conv[:, mode_count:]

    share = mode_count**3 // devices
    padded = -(-share // 128) * 128
    conv = conv.T.reshape(devices, share)
    conv = jnp.pad(conv, ((0, 0), (0, padded - share))).reshape(devices, padded // 128, 128)
    extra = jnp.broadcast_to(
        diss.reshape(1, mode_count * mode_count // 128, 128), (devices, mode_count**2 // 128, 128)
    )
    packed = jnp.concatenate([conv, extra], axis=1).astype(bf16)
    moved = lax.all_to_all(packed, ("mode", "slab"), 0, 0, tiled=True)
    summed = moved.astype(f32).sum(0)
    total_cells = cells * rows_y * planes * slabs
    convective = summed[: padded // 128].reshape(padded)[:share].reshape(-1, mode_count)
    dissipation = summed[padded // 128 :].reshape(mode_count, mode_count)
    return (
        convective * (1.0 / math.sqrt(total_cells)),
        dissipation * (viscosity / total_cells),
    )


def solution(mesh):
    placed = (P("mode", None, "slab", None, None), P(None, ("mode", "slab"), None))
    return jax.shard_map(
        per_device,
        mesh=mesh,
        in_specs=placed,
        out_specs=(P(("mode", "slab"), None), P()),
        check_vma=False,
    )
```

```python
import functools
import math

import jax
import jax.numpy as jnp
from jax import lax
from jax.experimental import pallas as pl
from jax.experimental.pallas import tpu as pltpu
from jax.sharding import PartitionSpec as P

viscosity = 0.05
bf16 = jnp.bfloat16
f32 = jnp.float32
MIB = 2**20
CUTS = (0.5,)
TIED = 2

vmem = pl.BlockSpec(memory_space=pltpu.VMEM)
smem = pl.BlockSpec(memory_space=pltpu.SMEM)


def spread(rows):
    return pltpu.VMEM(rows, f32)


def room(*arrays):
    size = sum(math.prod(array.shape) * jnp.dtype(array.dtype).itemsize for array in arrays)
    spare = 4 * MIB if size < 24 * MIB else 24 * MIB
    return pltpu.CompilerParams(vmem_limit_bytes=int(min(60 * MIB, 1.2 * size + spare)))


def cost(microseconds):
    return pl.CostEstimate(
        flops=int(1e9 * microseconds), bytes_accessed=int(3e6 * microseconds), transcendentals=0
    )


def dot_last(left, right, **options):
    return lax.dot_general(
        left, right, (((1,), (1,)), ((), ())), preferred_element_type=f32, **options
    )


def head_kernel(sizes, me_ref, modes_ref, *refs):
    owners, spans = sizes
    *outs, turned = refs
    local, comps, planes, rows_y, cells = modes_ref.shape
    lanes = planes * rows_y
    per_cell = comps * local
    pieces = lanes // 128
    unit = (
        lax.broadcasted_iota(jnp.int32, (cells, cells), 0)
        == lax.broadcasted_iota(jnp.int32, (cells, cells), 1)
    ).astype(f32)
    unit = unit.astype(bf16)
    for comp in range(comps):
        for mode in range(local):
            field = modes_ref[mode, comp].reshape(lanes, cells)
            flipped = dot_last(unit, field)
            for piece in range(pieces):
                turned[piece, pl.ds(comp * local + mode, cells, stride=per_cell), :] = flipped[
                    :, piece * 128 : (piece + 1) * 128
                ]
    pairs = cells // 2 // owners
    for number, out in enumerate(outs):
        start, stop = spans[number // owners]
        target = me_ref[0] ^ (number % owners)
        for row in range(start, stop):
            pair = lax.rem(target * pairs + (row + cells // 2), cells // 2)
            first = pl.multiple_of(pair * (2 * per_cell), math.gcd(2 * per_cell, 8))
            for piece in range(pieces):
                out[row - start, :, piece * 128 : (piece + 1) * 128] = turned[
                    piece, pl.ds(first, 2 * per_cell), :
                ].astype(bf16)


def head(me, modes, owners, spans):
    local, comps, planes, rows_y, cells = modes.shape
    lanes = planes * rows_y
    height = 2 * comps * local
    shapes = [
        jax.ShapeDtypeStruct((stop - start, height, lanes), bf16)
        for start, stop in spans
        for unused in range(owners)
    ]
    turned = spread((lanes // 128, cells * comps * local, 128))
    results = pl.pallas_call(
        functools.partial(head_kernel, (owners, spans)),
        in_specs=[smem, vmem],
        out_specs=[vmem] * len(shapes),
        out_shape=shapes,
        scratch_shapes=[turned],
        compiler_params=room(modes, turned, *shapes),
        cost_estimate=cost(1.0),
        name="head",
    )(me, modes)
    return [results[q * owners : (q + 1) * owners] for q in range(len(spans))]


def pack_kernel(owners, planes, volume_ref, after_ref, out_ref):
    rows, cells = volume_ref.shape[1:]
    slabs = out_ref.shape[0] // owners
    depth = cells // owners
    by_slab = volume_ref[...].reshape(slabs, planes, rows, cells)
    for owner in range(owners):
        out_ref[owner * slabs : (owner + 1) * slabs, :] = jnp.concatenate(
            [
                by_slab[:, plane, row, owner * depth : (owner + 1) * depth]
                for plane in range(planes)
                for row in range(rows)
            ],
            axis=1,
        )


def pack(volume, after, owners, planes):
    devices = owners * (volume.shape[0] // planes)
    out_shape = jax.ShapeDtypeStruct((devices, volume.size // devices), f32)
    return pl.pallas_call(
        functools.partial(pack_kernel, owners, planes),
        in_specs=[vmem, pl.BlockSpec(memory_space=pl.ANY)],
        out_specs=vmem,
        out_shape=out_shape,
        compiler_params=room(volume, out_shape),
        cost_estimate=cost(0.3),
        name="pack",
    )(volume, after)


def assemble_kernel(edge, me_ref, *refs):
    *blocks, out_ref, edge_ref, wide = refs
    local = blocks[0].shape[1] // 6
    total = local * len(blocks)
    rows = blocks[0].shape[0]
    place = 0
    for row in range(rows):
        for shift, block in enumerate(blocks):
            first = (me_ref[0] ^ shift) * local
            values = block[row].astype(f32)
            for part in range(6):
                for piece in range(wide.shape[1]):
                    wide[row, piece, pl.ds(part * total + first, local), :] = values[
                        part * local : (part + 1) * local, piece * 128 : (piece + 1) * 128
                    ]
    for row in range(rows):
        for piece in range(wide.shape[1]):
            lanes = slice(piece * 128, (piece + 1) * 128)
            merged = wide[row, piece].astype(bf16)
            if row == edge:
                edge_ref[0, :, lanes] = merged
            else:
                out_ref[place, :, lanes] = merged
        place += row != edge


def assemble(me, blocks, edge):
    rows, height, lanes = blocks[0].shape
    height *= len(blocks)
    body = rows - (edge is not None)
    wide = spread((rows, lanes // 128, height, 128))
    out_shape = (
        jax.ShapeDtypeStruct((body, height, lanes), bf16),
        jax.ShapeDtypeStruct((1, height, lanes), bf16),
    )
    return pl.pallas_call(
        functools.partial(assemble_kernel, edge),
        in_specs=[smem] + [vmem] * len(blocks),
        out_specs=(vmem, vmem),
        out_shape=out_shape,
        scratch_shapes=[wide],
        compiler_params=room(wide, *blocks, *out_shape),
        cost_estimate=cost(0.2),
        name="assemble",
    )(me, *blocks)


def central(first, second, fourth, fifth):
    return ((first - fifth) * (1.0 / 12.0) + (fourth - second) * (8.0 / 12.0)).astype(bf16)


def repack(ref, out, groups):
    rows = [ref[pl.ds(number, groups, stride=8), :][:, :48] for number in range(8)]
    out[pl.ds(0, groups, stride=3), :] = jnp.concatenate(
        [rows[0], rows[1], rows[2][:, :32]], axis=1
    )
    out[pl.ds(1, groups, stride=3), :] = jnp.concatenate(
        [rows[2][:, 32:], rows[3], rows[4], rows[5][:, :16]], axis=1
    )
    out[pl.ds(2, groups, stride=3), :] = jnp.concatenate(
        [rows[5][:, 16:], rows[6], rows[7]], axis=1
    )


def unpack(ref, first, groups):
    wide = [ref[pl.ds(first + number, groups, stride=3), :] for number in range(3)]
    return [
        wide[0][:, :48],
        wide[0][:, 48:96],
        jnp.concatenate([wide[0][:, 96:], wide[1][:, :16]], axis=1),
        wide[1][:, 16:64],
        wide[1][:, 64:112],
        jnp.concatenate([wide[1][:, 112:], wide[2][:, :32]], axis=1),
        wide[2][:, 32:80],
        wide[2][:, 80:],
    ]


def galerkin_kernel(field_plan, halo_plan, has_sum, packs, rows_y, depth, core_ref, *refs):
    count = len(halo_plan)
    refs = list(refs)
    conv_in, diss_in = (refs.pop(0), refs.pop(0)) if has_sum else (None, None)
    volume_ref = refs.pop(0)
    if refs[-2].shape != refs[-1].shape:
        refs.append(refs[-1])
    fields, low, high, weights_ref, carried0, carried1 = refs[-6:]
    buffers = (refs[-14:-10], refs[-10:-6])
    if packs:
        flat, packed_diss, diss_ref, conv_ref = refs[-18:-14]
        message_ref = refs[-19]
        sources = refs[:-19]
    else:
        conv_ref, diss_ref = refs[-16:-14]
        sources = refs[:-16]
    height, lanes = fields.shape[1:]
    half = height // 2
    mode_count = half // 3
    width = 2 * lanes

    for slot, (operand, row) in enumerate(field_plan):
        fields[slot] = sources[operand][row]
    odd_core = core_ref[0] == 1

    def fill(lower, upper):
        for slot, (inter, intra, row, unused) in enumerate(halo_plan):
            lower[slot] = sources[inter][row]
            upper[slot] = sources[intra][row]

    @pl.when(odd_core)
    def odd():
        fill(high, low)

    @pl.when(jnp.logical_not(odd_core))
    def even():
        fill(low, high)

    if has_sum:
        conv_ref[...] = conv_in[...]
        diss_ref[...] = diss_in[...]
    else:
        conv_ref[...] = jnp.zeros_like(conv_ref)
        diss_ref[...] = jnp.zeros_like(diss_ref)

    devices = volume_ref.shape[0]
    rows = rows_y // devices
    lane = lax.broadcasted_iota(jnp.int32, (devices, lanes), 1)
    device = lax.broadcasted_iota(jnp.int32, (devices, lanes), 0)
    weights = jnp.zeros((depth, lanes), f32)
    for plane in range(lanes // rows_y):
        for row in range(rows):
            place = (plane * rows + row) * depth
            chosen = (lane == plane * rows_y + device * rows + row).astype(f32)
            weights += lax.dot_general(
                volume_ref[:, place : place + depth],
                chosen,
                (((0,), (0,)), ((), ())),
                preferred_element_type=f32,
                precision=lax.Precision.HIGHEST,
            )
    weights_ref[...] = weights
    for buffer in buffers:
        buffer[3][2 * mode_count :, :] = jnp.zeros_like(buffer[3][2 * mode_count :, :])
        buffer[1][mode_count:, :] = jnp.zeros_like(buffer[1][mode_count:, :])

    row_y = lax.broadcasted_iota(jnp.int32, (height, lanes), 1) % rows_y

    def shifted(array, step):
        moved = pltpu.roll(array, (-step) % lanes, 1)
        inside = (row_y + step >= 0) & (row_y + step < rows_y)
        return jnp.where(inside, moved, 0.0)

    first_cell = halo_plan[0][3]

    def gradients(step, buffer):
        slopes, scaled, values, stationary = buffer
        before = fields[step].astype(f32)
        here = fields[step + 1].astype(f32)
        after = fields[step + 2].astype(f32)
        left = low[step].astype(f32)
        right = high[step].astype(f32)
        along_x = central(
            left,
            jnp.concatenate([left[:, rows_y:], here[:, : lanes - rows_y]], axis=1),
            jnp.concatenate([here[:, rows_y:], right[:, : lanes - rows_y]], axis=1),
            right,
        )
        along_y = central(shifted(here, -2), shifted(here, -1), shifted(here, 1), shifted(here, 2))
        along_z = jnp.concatenate(
            [
                central(before[:half], before[half:], here[half:], after[:half]),
                central(before[half:], here[:half], after[:half], after[half:]),
            ],
            axis=0,
        )
        for parity in range(2):
            span = slice(parity * lanes, (parity + 1) * lanes)
            own = slice(parity * half, (parity + 1) * half)
            weights = weights_ref[pl.ds(2 * (first_cell + step) + parity, 1), :]
            values[:, span] = fields[step + 1, own, :]
            product = here[own] * weights
            coarse = product.astype(bf16)
            fine = (product - coarse.astype(f32)).astype(bf16)
            for comp in range(3):
                modes = slice(comp * mode_count, (comp + 1) * mode_count)
                place = slice((2 * comp + parity) * lanes, (2 * comp + parity + 1) * lanes)
                stationary[:mode_count, place] = coarse[modes]
                stationary[mode_count : 2 * mode_count, place] = fine[modes]
                for direction, along in enumerate((along_x, along_y, along_z)):
                    number = comp * 3 + direction
                    begin = parity * half + comp * mode_count
                    piece = along[begin : begin + mode_count]
                    slopes[number * mode_count : (number + 1) * mode_count, span] = piece
                    begin = number * width + parity * lanes
                    scaled[:mode_count, begin : begin + lanes] = (piece.astype(f32) * weights).astype(bf16)

    def contract(buffer, carried):
        slopes, scaled, values, stationary = buffer
        side = jnp.concatenate(
            [slopes[number * mode_count : (number + 1) * mode_count, :] for number in range(9)],
            axis=1,
        )
        diss_ref[...] += dot_last(side, scaled[...])
        for j in range(mode_count):
            rows = [
                jnp.broadcast_to(
                    values[b * mode_count + j : b * mode_count + j + 1, :], (mode_count, width)
                )
                for b in range(3)
            ]
            for a in range(3):
                parts = [
                    slopes[(a * 3 + b) * mode_count : (a * 3 + b + 1) * mode_count, :]
                    for b in range(3)
                ]
                carried[j * mode_count : (j + 1) * mode_count, a * width : (a + 1) * width] = (
                    rows[0] * parts[0] + rows[1] * parts[1] + rows[2] * parts[2]
                )
        conv_ref[...] += dot_last(carried[...], stationary[...])

    gradients(0, buffers[0])

    def two_steps(number, unused):
        gradients(2 * number + 1, buffers[1])
        contract(buffers[0], carried0)
        gradients(jnp.minimum(2 * number + 2, count - 1), buffers[0])
        contract(buffers[1], carried1)
        return unused

    lax.fori_loop(0, count // 2, two_steps, 0)
    if count % 2:
        contract(buffers[0], carried0)

    if packs:
        chunks = mode_count * mode_count // 128
        for chunk in range(chunks):
            part = conv_ref[chunk * 128 : (chunk + 1) * 128, :].T
            flat[pl.ds(chunk, mode_count, stride=chunks), :] = (
                part[:mode_count] + part[mode_count : 2 * mode_count]
            )
        repack(diss_ref, packed_diss, mode_count // 8)
        devices, total, unused = message_ref.shape
        share = total - packed_diss.shape[0]
        tail = packed_diss[...]
        for device in range(devices):
            message_ref[device] = jnp.concatenate(
                [flat[device * share : (device + 1) * share, :], tail], axis=0
            ).astype(bf16)


def galerkin(core, sums, volume, sources, field_plan, halo_plan, rows_y, depth, message):
    height, lanes = sources[0].shape[1:]
    mode_count = height // 6
    used = sorted({e[0] for e in field_plan} | {o for e in halo_plan for o in e[:2]})
    number = {operand: place for place, operand in enumerate(used)}
    field_plan = tuple((number[operand], row) for operand, row in field_plan)
    halo_plan = tuple((number[p], number[q], row, cell) for p, q, row, cell in halo_plan)
    operands = list(sums or ()) + [volume] + [sources[operand] for operand in used]
    square = mode_count * mode_count
    scratch = []
    if message is None:
        out_shape = (
            jax.ShapeDtypeStruct((square, 128), f32),
            jax.ShapeDtypeStruct((mode_count, 128), f32),
        )
    else:
        out_shape = jax.ShapeDtypeStruct(message, bf16)
        scratch = [
            pltpu.VMEM((mode_count * square // 128, 128), f32),
            pltpu.VMEM((square // 128, 128), f32),
            pltpu.VMEM((mode_count, 128), f32),
            pltpu.VMEM((square, 128), f32),
        ]
    buffers = [
        pltpu.VMEM((9 * mode_count, 2 * lanes), bf16),
        pltpu.VMEM((128, 18 * lanes), bf16),
        pltpu.VMEM((3 * mode_count, 2 * lanes), bf16),
        pltpu.VMEM((128, 6 * lanes), bf16),
    ]
    scratch += (
        buffers
        + buffers
        + [
            pltpu.VMEM((len(field_plan), height, lanes), bf16),
            pltpu.VMEM((len(halo_plan), height, lanes), bf16),
            pltpu.VMEM((len(halo_plan), height, lanes), bf16),
            pltpu.VMEM((depth, lanes), f32),
        ]
        + [pltpu.VMEM((square, 6 * lanes), bf16)] * (2 if lanes <= 128 else 1)
    )
    shapes = out_shape if message is None else (out_shape,)
    return pl.pallas_call(
        functools.partial(
            galerkin_kernel, field_plan, halo_plan, sums is not None, message is not None, rows_y,
            depth,
        ),
        in_specs=[smem] + [vmem] * len(operands),
        out_specs=vmem if message is not None else (vmem, vmem),
        out_shape=out_shape,
        scratch_shapes=scratch,
        compiler_params=room(*operands, *shapes, *scratch),
        cost_estimate=cost(1.4 * len(halo_plan) + 0.5),
        name="galerkin",
    )(core, *operands)


def finish_kernel(scales, moved_ref, conv_ref, diss_ref, total):
    total[...] = jnp.sum(moved_ref[...].astype(f32), axis=0)
    groups = conv_ref.shape[0] // 8
    for number, rows in enumerate(unpack(total, 0, groups)):
        conv_ref[pl.ds(number, groups, stride=8), :] = rows * scales[0]
    first = 3 * groups
    groups = diss_ref.shape[0] // 8
    for number, rows in enumerate(unpack(total, first, groups)):
        diss_ref[pl.ds(number, groups, stride=8), :] = rows * scales[1]


def finish(moved, mode_count, scales):
    devices = moved.shape[0]
    return pl.pallas_call(
        functools.partial(finish_kernel, scales),
        in_specs=[vmem],
        out_specs=(vmem, vmem),
        out_shape=(
            jax.ShapeDtypeStruct((mode_count * mode_count // devices, mode_count), f32),
            jax.ShapeDtypeStruct((mode_count, mode_count), f32),
        ),
        scratch_shapes=[pltpu.VMEM(moved.shape[1:], f32)],
        compiler_params=room(moved, jax.ShapeDtypeStruct(moved.shape, f32)),
        cost_estimate=cost(0.8),
        name="finish",
    )(moved)


def per_device(modes, volume):
    local, comps, planes, rows_y, cells = modes.shape
    owners = lax.axis_size("mode")
    slabs = lax.axis_size("slab")
    devices = owners * slabs
    mode_count = local * owners
    lanes = planes * rows_y
    pairs = cells // 2 // owners
    me = lax.axis_index("mode").astype(jnp.int32).reshape(1)
    position = (lax.axis_index("slab") % 2).astype(jnp.int32).reshape(1)

    cuts = [0] + [int(pairs * cut) for cut in CUTS] + [pairs]
    chunks = len(cuts) - 1
    spans = tuple(
        (cuts[q] - (q == 0), cuts[q + 1] + (q == chunks - 1)) for q in range(chunks)
    )
    messages = head(me, modes, owners, spans)

    weights = pack(volume, messages[0][0], owners, planes)
    weights = lax.all_to_all(weights, ("mode", "slab"), 0, 0, tiled=True)

    def exchange(blocks):
        moved = [blocks[0]]
        for shift in range(1, owners):
            moved.append(
                lax.ppermute(
                    blocks[shift], "mode", [(source, source ^ shift) for source in range(owners)]
                )
            )
        return moved

    inter = [(i, i + 1) for i in range(1, slabs - 1, 2)]
    inter += [(j, i) for i, j in inter]
    intra = [(i, i ^ 1) for i in range(slabs)]

    sources = []
    for q in range(chunks):
        edge = 0 if q == 0 else (spans[q][1] - spans[q][0] - 1 if q == chunks - 1 else None)
        blocks = exchange(messages[q])
        body, edge_row = assemble(me, blocks, edge)
        between = lax.ppermute(body, "slab", inter)
        within = lax.ppermute(body, "slab", intra)
        sources += [body, edge_row, between, within]
        if q + 1 < chunks:
            tied = TIED
            *held, messages[q + 1] = lax.optimization_barrier((*blocks[1 : 1 + tied], messages[q + 1]))

    def place(row):
        if row < 0:
            return (1, 0)
        if row >= pairs:
            return (4 * chunks - 3, 0)
        q = max(q for q in range(chunks) if cuts[q] <= row)
        return (4 * q, row - cuts[q])

    sums = None
    share = mode_count**3 // devices
    fast = share % 384 == 0 and mode_count == 48
    message = (devices, (share + mode_count**2) // 128, 128) if fast else None
    for q in range(chunks):
        last = q == chunks - 1
        start = cuts[q] - (q > 0)
        stop = pairs if last else cuts[q + 1] - 1
        field_plan = [place(row) for row in range(start - 1, stop + 1)]
        halo_plan = []
        for row in range(start, stop):
            operand, inner = place(row)
            halo_plan.append((operand + 2, operand + 3, inner, row))
        sums = galerkin(
            position, sums, weights, sources, field_plan, halo_plan, rows_y,
            cells // owners, message if last else None,
        )

    total_cells = cells * rows_y * planes * slabs
    scales = (1.0 / math.sqrt(total_cells), viscosity / total_cells)
    if fast:
        moved = lax.all_to_all(sums, ("mode", "slab"), 0, 0, tiled=True)
        return finish(moved, mode_count, scales)
    conv, diss = sums
    conv = conv[:, :mode_count] + conv[:, mode_count : 2 * mode_count]
    padded = -(-share // 128) * 128
    conv = conv.T.reshape(devices, share)
    conv = jnp.pad(conv, ((0, 0), (0, padded - share))).reshape(devices, padded // 128, 128)
    extra = jnp.broadcast_to(
        diss[:, :mode_count].reshape(1, -1, 128), (devices, mode_count**2 // 128, 128)
    )
    packed = jnp.concatenate([conv, extra], axis=1).astype(bf16)
    moved = lax.all_to_all(packed, ("mode", "slab"), 0, 0, tiled=True).astype(f32).sum(0)
    convective = moved[: padded // 128].reshape(padded)[:share].reshape(-1, mode_count)
    dissipation = moved[padded // 128 :].reshape(mode_count, mode_count)
    return (convective * scales[0], dissipation * scales[1])


def solution(mesh):
    placed = (P("mode", None, "slab", None, None), P(None, ("mode", "slab"), None))
    return jax.shard_map(
        per_device,
        mesh=mesh,
        in_specs=placed,
        out_specs=(P(("mode", "slab"), None), P()),
        check_vma=False,
    )
```

```python
import functools
import math

import jax
import jax.numpy as jnp
from jax import lax
from jax.experimental import pallas as pl
from jax.experimental.pallas import tpu as pltpu
from jax.sharding import PartitionSpec as P

viscosity = 0.05
bf16 = jnp.bfloat16
f32 = jnp.float32
MIB = 2**20
CUTS = (0.5625,)

vmem = pl.BlockSpec(memory_space=pltpu.VMEM)
smem = pl.BlockSpec(memory_space=pltpu.SMEM)


def spread(rows):
    return pltpu.VMEM(rows, f32)


def room(*arrays):
    size = sum(math.prod(array.shape) * jnp.dtype(array.dtype).itemsize for array in arrays)
    spare = 4 * MIB if size < 24 * MIB else 24 * MIB
    return pltpu.CompilerParams(vmem_limit_bytes=int(min(60 * MIB, 1.2 * size + spare)))


def cost(microseconds):
    return pl.CostEstimate(
        flops=int(1e9 * microseconds), bytes_accessed=int(3e6 * microseconds), transcendentals=0
    )


def dot_last(left, right, **options):
    return lax.dot_general(
        left, right, (((1,), (1,)), ((), ())), preferred_element_type=f32, **options
    )


def head_kernel(sizes, me_ref, modes_ref, *refs):
    owners, spans = sizes
    *outs, turned = refs
    local, comps, planes, rows_y, cells = modes_ref.shape
    lanes = planes * rows_y
    per_cell = comps * local
    pieces = lanes // 128
    unit = (
        lax.broadcasted_iota(jnp.int32, (cells, cells), 0)
        == lax.broadcasted_iota(jnp.int32, (cells, cells), 1)
    ).astype(f32)
    unit = unit.astype(bf16)
    for comp in range(comps):
        for mode in range(local):
            field = modes_ref[mode, comp].reshape(lanes, cells)
            flipped = dot_last(unit, field)
            for piece in range(pieces):
                turned[piece, pl.ds(comp * local + mode, cells, stride=per_cell), :] = flipped[
                    :, piece * 128 : (piece + 1) * 128
                ]
    pairs = cells // 2 // owners
    for number, out in enumerate(outs):
        start, stop = spans[number // owners]
        target = me_ref[0] ^ (number % owners)
        for row in range(start, stop):
            pair = lax.rem(target * pairs + (row + cells // 2), cells // 2)
            first = pl.multiple_of(pair * (2 * per_cell), math.gcd(2 * per_cell, 8))
            for piece in range(pieces):
                out[row - start, :, piece * 128 : (piece + 1) * 128] = turned[
                    piece, pl.ds(first, 2 * per_cell), :
                ].astype(bf16)


def head(me, modes, owners, spans):
    local, comps, planes, rows_y, cells = modes.shape
    lanes = planes * rows_y
    height = 2 * comps * local
    shapes = [
        jax.ShapeDtypeStruct((stop - start, height, lanes), bf16)
        for start, stop in spans
        for unused in range(owners)
    ]
    turned = spread((lanes // 128, cells * comps * local, 128))
    results = pl.pallas_call(
        functools.partial(head_kernel, (owners, spans)),
        in_specs=[smem, vmem],
        out_specs=[vmem] * len(shapes),
        out_shape=shapes,
        scratch_shapes=[turned],
        compiler_params=room(modes, turned, *shapes),
        cost_estimate=cost(1.0),
        name="head",
    )(me, modes)
    return [results[q * owners : (q + 1) * owners] for q in range(len(spans))]


def pack_kernel(owners, planes, volume_ref, after_ref, out_ref):
    rows, cells = volume_ref.shape[1:]
    slabs = out_ref.shape[0] // owners
    depth = cells // owners
    by_slab = volume_ref[...].reshape(slabs, planes, rows, cells)
    for owner in range(owners):
        out_ref[owner * slabs : (owner + 1) * slabs, :] = jnp.concatenate(
            [
                by_slab[:, plane, row, owner * depth : (owner + 1) * depth]
                for plane in range(planes)
                for row in range(rows)
            ],
            axis=1,
        )


def pack(volume, after, owners, planes):
    devices = owners * (volume.shape[0] // planes)
    out_shape = jax.ShapeDtypeStruct((devices, volume.size // devices), f32)
    return pl.pallas_call(
        functools.partial(pack_kernel, owners, planes),
        in_specs=[vmem, pl.BlockSpec(memory_space=pl.ANY)],
        out_specs=vmem,
        out_shape=out_shape,
        compiler_params=room(volume, out_shape),
        cost_estimate=cost(0.3),
        name="pack",
    )(volume, after)


def assemble_kernel(edge, me_ref, *refs):
    *blocks, out_ref, edge_ref, wide = refs
    local = blocks[0].shape[1] // 6
    total = local * len(blocks)
    rows = blocks[0].shape[0]
    place = 0
    for row in range(rows):
        for shift, block in enumerate(blocks):
            first = (me_ref[0] ^ shift) * local
            values = block[row].astype(f32)
            for part in range(6):
                for piece in range(wide.shape[1]):
                    wide[row, piece, pl.ds(part * total + first, local), :] = values[
                        part * local : (part + 1) * local, piece * 128 : (piece + 1) * 128
                    ]
    for row in range(rows):
        for piece in range(wide.shape[1]):
            lanes = slice(piece * 128, (piece + 1) * 128)
            merged = wide[row, piece].astype(bf16)
            if row == edge:
                edge_ref[0, :, lanes] = merged
            else:
                out_ref[place, :, lanes] = merged
        place += row != edge


def assemble(me, blocks, edge):
    rows, height, lanes = blocks[0].shape
    height *= len(blocks)
    body = rows - (edge is not None)
    wide = spread((rows, lanes // 128, height, 128))
    out_shape = (
        jax.ShapeDtypeStruct((body, height, lanes), bf16),
        jax.ShapeDtypeStruct((1, height, lanes), bf16),
    )
    return pl.pallas_call(
        functools.partial(assemble_kernel, edge),
        in_specs=[smem] + [vmem] * len(blocks),
        out_specs=(vmem, vmem),
        out_shape=out_shape,
        scratch_shapes=[wide],
        compiler_params=room(wide, *blocks, *out_shape),
        cost_estimate=cost(0.2),
        name="assemble",
    )(me, *blocks)


def central(first, second, fourth, fifth):
    return ((first - fifth) * (1.0 / 12.0) + (fourth - second) * (8.0 / 12.0)).astype(bf16)


def repack(ref, out, groups):
    rows = [ref[pl.ds(number, groups, stride=8), :][:, :48] for number in range(8)]
    out[pl.ds(0, groups, stride=3), :] = jnp.concatenate(
        [rows[0], rows[1], rows[2][:, :32]], axis=1
    )
    out[pl.ds(1, groups, stride=3), :] = jnp.concatenate(
        [rows[2][:, 32:], rows[3], rows[4], rows[5][:, :16]], axis=1
    )
    out[pl.ds(2, groups, stride=3), :] = jnp.concatenate(
        [rows[5][:, 16:], rows[6], rows[7]], axis=1
    )


def unpack(ref, first, groups):
    wide = [ref[pl.ds(first + number, groups, stride=3), :] for number in range(3)]
    return [
        wide[0][:, :48],
        wide[0][:, 48:96],
        jnp.concatenate([wide[0][:, 96:], wide[1][:, :16]], axis=1),
        wide[1][:, 16:64],
        wide[1][:, 64:112],
        jnp.concatenate([wide[1][:, 112:], wide[2][:, :32]], axis=1),
        wide[2][:, 32:80],
        wide[2][:, 80:],
    ]


def galerkin_kernel(field_plan, halo_plan, has_sum, packs, rows_y, depth, core_ref, *refs):
    count = len(halo_plan)
    refs = list(refs)
    conv_in, diss_in = (refs.pop(0), refs.pop(0)) if has_sum else (None, None)
    volume_ref = refs.pop(0)
    if refs[-2].shape != refs[-1].shape:
        refs.append(refs[-1])
    fields, low, high, weights_ref, carried0, carried1 = refs[-6:]
    buffers = (refs[-14:-10], refs[-10:-6])
    if packs:
        flat, packed_diss, diss_ref, conv_ref = refs[-18:-14]
        message_ref = refs[-19]
        sources = refs[:-19]
    else:
        conv_ref, diss_ref = refs[-16:-14]
        sources = refs[:-16]
    height, lanes = fields.shape[1:]
    half = height // 2
    mode_count = half // 3
    width = 2 * lanes

    for slot, (operand, row) in enumerate(field_plan):
        fields[slot] = sources[operand][row]
    odd_core = core_ref[0] == 1

    def fill(lower, upper):
        for slot, (inter, intra, row, unused) in enumerate(halo_plan):
            lower[slot] = sources[inter][row]
            upper[slot] = sources[intra][row]

    @pl.when(odd_core)
    def odd():
        fill(high, low)

    @pl.when(jnp.logical_not(odd_core))
    def even():
        fill(low, high)

    if has_sum:
        conv_ref[...] = conv_in[...]
        diss_ref[...] = diss_in[...]
    else:
        conv_ref[...] = jnp.zeros_like(conv_ref)
        diss_ref[...] = jnp.zeros_like(diss_ref)

    devices = volume_ref.shape[0]
    rows = rows_y // devices
    lane = lax.broadcasted_iota(jnp.int32, (devices, lanes), 1)
    device = lax.broadcasted_iota(jnp.int32, (devices, lanes), 0)
    weights = jnp.zeros((depth, lanes), f32)
    for plane in range(lanes // rows_y):
        for row in range(rows):
            place = (plane * rows + row) * depth
            chosen = (lane == plane * rows_y + device * rows + row).astype(f32)
            weights += lax.dot_general(
                volume_ref[:, place : place + depth],
                chosen,
                (((0,), (0,)), ((), ())),
                preferred_element_type=f32,
                precision=lax.Precision.HIGHEST,
            )
    weights_ref[...] = weights
    for buffer in buffers:
        buffer[3][2 * mode_count :, :] = jnp.zeros_like(buffer[3][2 * mode_count :, :])
        buffer[1][mode_count:, :] = jnp.zeros_like(buffer[1][mode_count:, :])

    row_y = lax.broadcasted_iota(jnp.int32, (height, lanes), 1) % rows_y

    def shifted(array, step):
        moved = pltpu.roll(array, (-step) % lanes, 1)
        inside = (row_y + step >= 0) & (row_y + step < rows_y)
        return jnp.where(inside, moved, 0.0)

    first_cell = halo_plan[0][3]

    def gradients(step, buffer):
        slopes, scaled, values, stationary = buffer
        before = fields[step].astype(f32)
        here = fields[step + 1].astype(f32)
        after = fields[step + 2].astype(f32)
        left = low[step].astype(f32)
        right = high[step].astype(f32)
        along_x = central(
            left,
            jnp.concatenate([left[:, rows_y:], here[:, : lanes - rows_y]], axis=1),
            jnp.concatenate([here[:, rows_y:], right[:, : lanes - rows_y]], axis=1),
            right,
        )
        along_y = central(shifted(here, -2), shifted(here, -1), shifted(here, 1), shifted(here, 2))
        along_z = jnp.concatenate(
            [
                central(before[:half], before[half:], here[half:], after[:half]),
                central(before[half:], here[:half], after[:half], after[half:]),
            ],
            axis=0,
        )
        for parity in range(2):
            span = slice(parity * lanes, (parity + 1) * lanes)
            own = slice(parity * half, (parity + 1) * half)
            weights = weights_ref[pl.ds(2 * (first_cell + step) + parity, 1), :]
            values[:, span] = fields[step + 1, own, :]
            product = here[own] * weights
            coarse = product.astype(bf16)
            fine = (product - coarse.astype(f32)).astype(bf16)
            for comp in range(3):
                modes = slice(comp * mode_count, (comp + 1) * mode_count)
                place = slice((2 * comp + parity) * lanes, (2 * comp + parity + 1) * lanes)
                stationary[:mode_count, place] = coarse[modes]
                stationary[mode_count : 2 * mode_count, place] = fine[modes]
                for direction, along in enumerate((along_x, along_y, along_z)):
                    number = comp * 3 + direction
                    begin = parity * half + comp * mode_count
                    piece = along[begin : begin + mode_count]
                    slopes[number * mode_count : (number + 1) * mode_count, span] = piece
                    begin = number * width + parity * lanes
                    scaled[:mode_count, begin : begin + lanes] = (piece.astype(f32) * weights).astype(bf16)

    def contract(buffer, carried):
        slopes, scaled, values, stationary = buffer
        side = jnp.concatenate(
            [slopes[number * mode_count : (number + 1) * mode_count, :] for number in range(9)],
            axis=1,
        )
        diss_ref[...] += dot_last(side, scaled[...])
        for j in range(mode_count):
            rows = [
                jnp.broadcast_to(
                    values[b * mode_count + j : b * mode_count + j + 1, :], (mode_count, width)
                )
                for b in range(3)
            ]
            for a in range(3):
                parts = [
                    slopes[(a * 3 + b) * mode_count : (a * 3 + b + 1) * mode_count, :]
                    for b in range(3)
                ]
                carried[j * mode_count : (j + 1) * mode_count, a * width : (a + 1) * width] = (
                    rows[0] * parts[0] + rows[1] * parts[1] + rows[2] * parts[2]
                )
        conv_ref[...] += dot_last(carried[...], stationary[...])

    gradients(0, buffers[0])

    def two_steps(number, unused):
        gradients(2 * number + 1, buffers[1])
        contract(buffers[0], carried0)
        gradients(jnp.minimum(2 * number + 2, count - 1), buffers[0])
        contract(buffers[1], carried1)
        return unused

    lax.fori_loop(0, count // 2, two_steps, 0)
    if count % 2:
        contract(buffers[0], carried0)

    if packs:
        chunks = mode_count * mode_count // 128
        for chunk in range(chunks):
            part = conv_ref[chunk * 128 : (chunk + 1) * 128, :].T
            flat[pl.ds(chunk, mode_count, stride=chunks), :] = (
                part[:mode_count] + part[mode_count : 2 * mode_count]
            )
        repack(diss_ref, packed_diss, mode_count // 8)
        devices, total, unused = message_ref.shape
        share = total - packed_diss.shape[0]
        tail = packed_diss[...]
        for device in range(devices):
            message_ref[device] = jnp.concatenate(
                [flat[device * share : (device + 1) * share, :], tail], axis=0
            ).astype(bf16)


def galerkin(core, sums, volume, sources, field_plan, halo_plan, rows_y, depth, message):
    height, lanes = sources[0].shape[1:]
    mode_count = height // 6
    used = sorted({e[0] for e in field_plan} | {o for e in halo_plan for o in e[:2]})
    number = {operand: place for place, operand in enumerate(used)}
    field_plan = tuple((number[operand], row) for operand, row in field_plan)
    halo_plan = tuple((number[p], number[q], row, cell) for p, q, row, cell in halo_plan)
    operands = list(sums or ()) + [volume] + [sources[operand] for operand in used]
    square = mode_count * mode_count
    scratch = []
    if message is None:
        out_shape = (
            jax.ShapeDtypeStruct((square, 128), f32),
            jax.ShapeDtypeStruct((mode_count, 128), f32),
        )
    else:
        out_shape = jax.ShapeDtypeStruct(message, bf16)
        scratch = [
            pltpu.VMEM((mode_count * square // 128, 128), f32),
            pltpu.VMEM((square // 128, 128), f32),
            pltpu.VMEM((mode_count, 128), f32),
            pltpu.VMEM((square, 128), f32),
        ]
    buffers = [
        pltpu.VMEM((9 * mode_count, 2 * lanes), bf16),
        pltpu.VMEM((128, 18 * lanes), bf16),
        pltpu.VMEM((3 * mode_count, 2 * lanes), bf16),
        pltpu.VMEM((128, 6 * lanes), bf16),
    ]
    scratch += (
        buffers
        + buffers
        + [
            pltpu.VMEM((len(field_plan), height, lanes), bf16),
            pltpu.VMEM((len(halo_plan), height, lanes), bf16),
            pltpu.VMEM((len(halo_plan), height, lanes), bf16),
            pltpu.VMEM((depth, lanes), f32),
        ]
        + [pltpu.VMEM((square, 6 * lanes), bf16)] * (2 if lanes <= 128 else 1)
    )
    shapes = out_shape if message is None else (out_shape,)
    return pl.pallas_call(
        functools.partial(
            galerkin_kernel, field_plan, halo_plan, sums is not None, message is not None, rows_y,
            depth,
        ),
        in_specs=[smem] + [vmem] * len(operands),
        out_specs=vmem if message is not None else (vmem, vmem),
        out_shape=out_shape,
        scratch_shapes=scratch,
        compiler_params=room(*operands, *shapes, *scratch),
        cost_estimate=cost(1.4 * len(halo_plan) + 0.5),
        name="galerkin",
    )(core, *operands)


def finish_kernel(scales, moved_ref, conv_ref, diss_ref, total, rows_ref):
    total[...] = jnp.sum(moved_ref[...].astype(f32), axis=0)
    groups = conv_ref.shape[1] // 8
    for number, rows in enumerate(unpack(total, 0, groups)):
        rows_ref[pl.ds(number, groups, stride=8), :] = rows * scales[0]
    conv_ref[...] = rows_ref[...].T
    first = 3 * groups
    groups = diss_ref.shape[0] // 8
    for number, rows in enumerate(unpack(total, first, groups)):
        diss_ref[pl.ds(number, groups, stride=8), :] = rows * scales[1]


def finish(moved, mode_count, scales):
    share = mode_count * mode_count // moved.shape[0]
    conv, diss = pl.pallas_call(
        functools.partial(finish_kernel, scales),
        in_specs=[vmem],
        out_specs=(vmem, vmem),
        out_shape=(
            jax.ShapeDtypeStruct((mode_count, share), f32),
            jax.ShapeDtypeStruct((mode_count, mode_count), f32),
        ),
        scratch_shapes=[
            pltpu.VMEM(moved.shape[1:], f32),
            pltpu.VMEM((share, mode_count), f32),
        ],
        compiler_params=room(moved, jax.ShapeDtypeStruct(moved.shape, f32)),
        name="finish",
    )(moved)
    return conv.T, diss


def per_device(modes, volume):
    local, comps, planes, rows_y, cells = modes.shape
    owners = lax.axis_size("mode")
    slabs = lax.axis_size("slab")
    devices = owners * slabs
    mode_count = local * owners
    lanes = planes * rows_y
    pairs = cells // 2 // owners
    me = lax.axis_index("mode").astype(jnp.int32).reshape(1)
    position = (lax.axis_index("slab") % 2).astype(jnp.int32).reshape(1)

    cuts = [0] + [int(pairs * cut) for cut in CUTS] + [pairs]
    chunks = len(cuts) - 1
    spans = tuple(
        (cuts[q] - (q == 0), cuts[q + 1] + (q == chunks - 1)) for q in range(chunks)
    )
    messages = head(me, modes, owners, spans)

    weights = pack(volume, messages[0][0], owners, planes)

    def exchange(blocks):
        moved = [blocks[0]]
        for shift in range(1, owners):
            moved.append(
                lax.ppermute(
                    blocks[shift], "mode", [(source, source ^ shift) for source in range(owners)]
                )
            )
        return moved

    inter = [(i, i + 1) for i in range(1, slabs - 1, 2)]
    inter += [(j, i) for i, j in inter]
    intra = [(i, i ^ 1) for i in range(slabs)]

    def after(value, *others):
        return lax.optimization_barrier((value, *others))[0]

    def place(row):
        if row < 0:
            return (1, 0)
        if row >= pairs:
            return (4 * chunks - 3, 0)
        q = max(q for q in range(chunks) if cuts[q] <= row)
        return (4 * q, row - cuts[q])

    share = mode_count**3 // devices
    fast = share % 384 == 0 and mode_count == 48
    message = (devices, (share + mode_count**2) // 128, 128) if fast else None

    def contraction(start, stop, sums, weights):
        last = stop == pairs
        field_plan = [place(row) for row in range(start - 1, stop + 1)]
        halo_plan = []
        for row in range(start, stop):
            operand, inner = place(row)
            halo_plan.append((operand + 2, operand + 3, inner, row))
        return galerkin(
            position, sums, weights, sources, field_plan, halo_plan, rows_y,
            cells // owners, message if last else None,
        )

    sources = []
    blocks = exchange(messages[0])
    for q in range(chunks):
        edge = 0 if q == 0 else (spans[q][1] - spans[q][0] - 1 if q == chunks - 1 else None)
        body, edge_row = assemble(me, blocks, edge)
        between = lax.ppermute(body, "slab", inter)
        within = lax.ppermute(body, "slab", intra)
        sources += [body, edge_row, between, within]
        if q == 0:
            weights = lax.all_to_all(after(weights, body), ("mode", "slab"), 0, 0, tiled=True)
        if q + 1 < chunks:
            blocks = exchange([after(message, *blocks[1:3]) for message in messages[q + 1]])

    sums = None
    done = 0
    for q in range(chunks):
        stop = pairs if q == chunks - 1 else cuts[q + 1] - 1
        sums = contraction(done, stop, sums, weights)
        done = stop

    total_cells = cells * rows_y * planes * slabs
    scales = (1.0 / math.sqrt(total_cells), viscosity / total_cells)
    if fast:
        moved = lax.all_to_all(sums, ("mode", "slab"), 0, 0, tiled=True)
        return finish(moved, mode_count, scales)
    conv, diss = sums
    conv = conv[:, :mode_count] + conv[:, mode_count : 2 * mode_count]
    padded = -(-share // 128) * 128
    conv = conv.T.reshape(devices, share)
    conv = jnp.pad(conv, ((0, 0), (0, padded - share))).reshape(devices, padded // 128, 128)
    extra = jnp.broadcast_to(
        diss[:, :mode_count].reshape(1, -1, 128), (devices, mode_count**2 // 128, 128)
    )
    packed = jnp.concatenate([conv, extra], axis=1).astype(bf16)
    moved = lax.all_to_all(packed, ("mode", "slab"), 0, 0, tiled=True).astype(f32).sum(0)
    convective = moved[: padded // 128].reshape(padded)[:share].reshape(-1, mode_count)
    dissipation = moved[padded // 128 :].reshape(mode_count, mode_count)
    return (convective * scales[0], dissipation * scales[1])


def solution(mesh):
    placed = (P("mode", None, "slab", None, None), P(None, ("mode", "slab"), None))
    return jax.shard_map(
        per_device,
        mesh=mesh,
        in_specs=placed,
        out_specs=(P(("mode", "slab"), None), P()),
        check_vma=False,
    )
```

```python
import functools
import math

import jax
import jax.numpy as jnp
from jax import lax
from jax.experimental import pallas as pl
from jax.experimental.pallas import tpu as pltpu
from jax.sharding import PartitionSpec as P

viscosity = 0.05
bf16 = jnp.bfloat16
f32 = jnp.float32
MIB = 2**20
CUTS = (0.5625,)

vmem = pl.BlockSpec(memory_space=pltpu.VMEM)
smem = pl.BlockSpec(memory_space=pltpu.SMEM)


def spread(rows):
    return pltpu.VMEM(rows, f32)


def room(*arrays):
    size = sum(math.prod(array.shape) * jnp.dtype(array.dtype).itemsize for array in arrays)
    spare = 4 * MIB if size < 24 * MIB else 24 * MIB
    return pltpu.CompilerParams(vmem_limit_bytes=int(min(60 * MIB, 1.2 * size + spare)))


def cost(microseconds):
    return pl.CostEstimate(
        flops=int(1e9 * microseconds), bytes_accessed=int(3e6 * microseconds), transcendentals=0
    )


def dot_last(left, right, **options):
    return lax.dot_general(
        left, right, (((1,), (1,)), ((), ())), preferred_element_type=f32, **options
    )


def head_kernel(sizes, me_ref, modes_ref, *refs):
    owners, spans = sizes
    *outs, turned = refs
    local, comps, planes, rows_y, cells = modes_ref.shape
    lanes = planes * rows_y
    per_cell = comps * local
    pieces = lanes // 128
    unit = (
        lax.broadcasted_iota(jnp.int32, (cells, cells), 0)
        == lax.broadcasted_iota(jnp.int32, (cells, cells), 1)
    ).astype(f32)
    unit = unit.astype(bf16)
    for comp in range(comps):
        for mode in range(local):
            field = modes_ref[mode, comp].reshape(lanes, cells)
            flipped = dot_last(unit, field)
            for piece in range(pieces):
                turned[piece, pl.ds(comp * local + mode, cells, stride=per_cell), :] = flipped[
                    :, piece * 128 : (piece + 1) * 128
                ]
    pairs = cells // 2 // owners
    for number, out in enumerate(outs):
        start, stop = spans[number // owners]
        target = me_ref[0] ^ (number % owners)
        for row in range(start, stop):
            pair = lax.rem(target * pairs + (row + cells // 2), cells // 2)
            first = pl.multiple_of(pair * (2 * per_cell), math.gcd(2 * per_cell, 8))
            for piece in range(pieces):
                out[row - start, :, piece * 128 : (piece + 1) * 128] = turned[
                    piece, pl.ds(first, 2 * per_cell), :
                ].astype(bf16)


def head(me, modes, owners, spans):
    local, comps, planes, rows_y, cells = modes.shape
    lanes = planes * rows_y
    height = 2 * comps * local
    shapes = [
        jax.ShapeDtypeStruct((stop - start, height, lanes), bf16)
        for start, stop in spans
        for unused in range(owners)
    ]
    turned = spread((lanes // 128, cells * comps * local, 128))
    results = pl.pallas_call(
        functools.partial(head_kernel, (owners, spans)),
        in_specs=[smem, vmem],
        out_specs=[vmem] * len(shapes),
        out_shape=shapes,
        scratch_shapes=[turned],
        compiler_params=room(modes, turned, *shapes),
        cost_estimate=cost(1.0),
        name="head",
    )(me, modes)
    return [results[q * owners : (q + 1) * owners] for q in range(len(spans))]


def pack_kernel(owners, planes, volume_ref, after_ref, out_ref):
    rows, cells = volume_ref.shape[1:]
    slabs = out_ref.shape[0] // owners
    depth = cells // owners
    by_slab = volume_ref[...].reshape(slabs, planes, rows, cells)
    for owner in range(owners):
        out_ref[owner * slabs : (owner + 1) * slabs, :] = jnp.concatenate(
            [
                by_slab[:, plane, row, owner * depth : (owner + 1) * depth]
                for plane in range(planes)
                for row in range(rows)
            ],
            axis=1,
        )


def pack(volume, after, owners, planes):
    devices = owners * (volume.shape[0] // planes)
    out_shape = jax.ShapeDtypeStruct((devices, volume.size // devices), f32)
    return pl.pallas_call(
        functools.partial(pack_kernel, owners, planes),
        in_specs=[vmem, pl.BlockSpec(memory_space=pl.ANY)],
        out_specs=vmem,
        out_shape=out_shape,
        compiler_params=room(volume, out_shape),
        cost_estimate=cost(0.3),
        name="pack",
    )(volume, after)


def assemble_kernel(edge, me_ref, *refs):
    *blocks, out_ref, edge_ref, wide = refs
    local = blocks[0].shape[1] // 6
    total = local * len(blocks)
    rows = blocks[0].shape[0]
    place = 0
    for row in range(rows):
        for shift, block in enumerate(blocks):
            first = (me_ref[0] ^ shift) * local
            values = block[row].astype(f32)
            for part in range(6):
                for piece in range(wide.shape[1]):
                    wide[row, piece, pl.ds(part * total + first, local), :] = values[
                        part * local : (part + 1) * local, piece * 128 : (piece + 1) * 128
                    ]
    for row in range(rows):
        for piece in range(wide.shape[1]):
            lanes = slice(piece * 128, (piece + 1) * 128)
            merged = wide[row, piece].astype(bf16)
            if row == edge:
                edge_ref[0, :, lanes] = merged
            else:
                out_ref[place, :, lanes] = merged
        place += row != edge


def assemble(me, blocks, edge):
    rows, height, lanes = blocks[0].shape
    height *= len(blocks)
    body = rows - (edge is not None)
    wide = spread((rows, lanes // 128, height, 128))
    out_shape = (
        jax.ShapeDtypeStruct((body, height, lanes), bf16),
        jax.ShapeDtypeStruct((1, height, lanes), bf16),
    )
    return pl.pallas_call(
        functools.partial(assemble_kernel, edge),
        in_specs=[smem] + [vmem] * len(blocks),
        out_specs=(vmem, vmem),
        out_shape=out_shape,
        scratch_shapes=[wide],
        compiler_params=room(wide, *blocks, *out_shape),
        cost_estimate=cost(0.2),
        name="assemble",
    )(me, *blocks)


def central(first, second, fourth, fifth):
    return ((first - fifth) * (1.0 / 12.0) + (fourth - second) * (8.0 / 12.0)).astype(bf16)


def halves(size):
    row = lax.broadcasted_iota(jnp.int32, (size, size), 0)
    column = lax.broadcasted_iota(jnp.int32, (size, size), 1)
    return row, column


def fold(square):
    half = square.shape[0] // 2
    row, column = halves(half)
    first, last = square[:half, :half], square[half:, half:]
    mixed = jnp.where(column >= row, first, last)
    diagonal = jnp.sum(jnp.where(column == row, last, 0.0), axis=1, keepdims=True)
    blank = jnp.zeros((half, 63 - 2 * half), f32)
    folded = jnp.concatenate([square[:half, half:], mixed, diagonal, blank], axis=1)
    return jnp.concatenate([folded[: half // 2], folded[half // 2 :]], axis=1)


def unfold(wide, size):
    half = size // 2
    row, column = halves(half)
    folded = jnp.concatenate([wide[:, :64], wide[:, 64:]], axis=0)
    cross = folded[:, :half]
    mixed = folded[:, half:size]
    turned = mixed.T
    first = jnp.where(column >= row, mixed, turned)
    last = jnp.where(column < row, mixed, turned)
    last = jnp.where(column == row, folded[:, size : size + 1], last)
    return jnp.concatenate(
        [
            jnp.concatenate([first, cross], axis=1),
            jnp.concatenate([cross.T, last], axis=1),
        ],
        axis=0,
    )


def unpack(ref, first, groups):
    wide = [ref[pl.ds(first + number, groups, stride=3), :] for number in range(3)]
    return [
        wide[0][:, :48],
        wide[0][:, 48:96],
        jnp.concatenate([wide[0][:, 96:], wide[1][:, :16]], axis=1),
        wide[1][:, 16:64],
        wide[1][:, 64:112],
        jnp.concatenate([wide[1][:, 112:], wide[2][:, :32]], axis=1),
        wide[2][:, 32:80],
        wide[2][:, 80:],
    ]


def galerkin_kernel(field_plan, halo_plan, has_sum, packs, rows_y, depth, core_ref, *refs):
    count = len(halo_plan)
    refs = list(refs)
    conv_in, diss_in = (refs.pop(0), refs.pop(0)) if has_sum else (None, None)
    volume_ref = refs.pop(0)
    if refs[-2].shape != refs[-1].shape:
        refs.append(refs[-1])
    fields, low, high, weights_ref, carried0, carried1 = refs[-6:]
    buffers = (refs[-14:-10], refs[-10:-6])
    if packs:
        flat, diss_ref, conv_ref = refs[-17:-14]
        message_ref = refs[-18]
        sources = refs[:-18]
    else:
        conv_ref, diss_ref = refs[-16:-14]
        sources = refs[:-16]
    height, lanes = fields.shape[1:]
    half = height // 2
    mode_count = half // 3
    width = 2 * lanes

    for slot, (operand, row) in enumerate(field_plan):
        fields[slot] = sources[operand][row]
    odd_core = core_ref[0] == 1

    def fill(lower, upper):
        for slot, (inter, intra, row, unused) in enumerate(halo_plan):
            lower[slot] = sources[inter][row]
            upper[slot] = sources[intra][row]

    @pl.when(odd_core)
    def odd():
        fill(high, low)

    @pl.when(jnp.logical_not(odd_core))
    def even():
        fill(low, high)

    if has_sum:
        conv_ref[...] = conv_in[...]
        diss_ref[...] = diss_in[...]
    else:
        conv_ref[...] = jnp.zeros_like(conv_ref)
        diss_ref[...] = jnp.zeros_like(diss_ref)

    devices = volume_ref.shape[0]
    rows = rows_y // devices
    lane = lax.broadcasted_iota(jnp.int32, (devices, lanes), 1)
    device = lax.broadcasted_iota(jnp.int32, (devices, lanes), 0)
    weights = jnp.zeros((depth, lanes), f32)
    for plane in range(lanes // rows_y):
        for row in range(rows):
            place = (plane * rows + row) * depth
            chosen = (lane == plane * rows_y + device * rows + row).astype(f32)
            weights += lax.dot_general(
                volume_ref[:, place : place + depth],
                chosen,
                (((0,), (0,)), ((), ())),
                preferred_element_type=f32,
                precision=lax.Precision.HIGHEST,
            )
    weights_ref[...] = weights
    for buffer in buffers:
        buffer[3][2 * mode_count :, :] = jnp.zeros_like(buffer[3][2 * mode_count :, :])
        buffer[1][mode_count:, :] = jnp.zeros_like(buffer[1][mode_count:, :])

    row_y = lax.broadcasted_iota(jnp.int32, (height, lanes), 1) % rows_y

    def shifted(array, step):
        moved = pltpu.roll(array, (-step) % lanes, 1)
        inside = (row_y + step >= 0) & (row_y + step < rows_y)
        return jnp.where(inside, moved, 0.0)

    first_cell = halo_plan[0][3]

    def gradients(step, buffer):
        slopes, scaled, values, stationary = buffer
        before = fields[step].astype(f32)
        here = fields[step + 1].astype(f32)
        after = fields[step + 2].astype(f32)
        left = low[step].astype(f32)
        right = high[step].astype(f32)
        along_x = central(
            left,
            jnp.concatenate([left[:, rows_y:], here[:, : lanes - rows_y]], axis=1),
            jnp.concatenate([here[:, rows_y:], right[:, : lanes - rows_y]], axis=1),
            right,
        )
        along_y = central(shifted(here, -2), shifted(here, -1), shifted(here, 1), shifted(here, 2))
        along_z = jnp.concatenate(
            [
                central(before[:half], before[half:], here[half:], after[:half]),
                central(before[half:], here[:half], after[:half], after[half:]),
            ],
            axis=0,
        )
        for parity in range(2):
            span = slice(parity * lanes, (parity + 1) * lanes)
            own = slice(parity * half, (parity + 1) * half)
            weights = weights_ref[pl.ds(2 * (first_cell + step) + parity, 1), :]
            values[:, span] = fields[step + 1, own, :]
            product = here[own] * weights
            coarse = product.astype(bf16)
            fine = (product - coarse.astype(f32)).astype(bf16)
            for comp in range(3):
                modes = slice(comp * mode_count, (comp + 1) * mode_count)
                place = slice((2 * comp + parity) * lanes, (2 * comp + parity + 1) * lanes)
                stationary[:mode_count, place] = coarse[modes]
                stationary[mode_count : 2 * mode_count, place] = fine[modes]
                for direction, along in enumerate((along_x, along_y, along_z)):
                    number = comp * 3 + direction
                    begin = parity * half + comp * mode_count
                    piece = along[begin : begin + mode_count]
                    slopes[number * mode_count : (number + 1) * mode_count, span] = piece
                    begin = number * width + parity * lanes
                    scaled[:mode_count, begin : begin + lanes] = (piece.astype(f32) * weights).astype(bf16)

    def contract(buffer, carried):
        slopes, scaled, values, stationary = buffer
        side = jnp.concatenate(
            [slopes[number * mode_count : (number + 1) * mode_count, :] for number in range(9)],
            axis=1,
        )
        diss_ref[...] += dot_last(side, scaled[...])
        for j in range(mode_count):
            rows = [
                jnp.broadcast_to(
                    values[b * mode_count + j : b * mode_count + j + 1, :], (mode_count, width)
                )
                for b in range(3)
            ]
            for a in range(3):
                parts = [
                    slopes[(a * 3 + b) * mode_count : (a * 3 + b + 1) * mode_count, :]
                    for b in range(3)
                ]
                carried[j * mode_count : (j + 1) * mode_count, a * width : (a + 1) * width] = (
                    rows[0] * parts[0] + rows[1] * parts[1] + rows[2] * parts[2]
                )
        conv_ref[...] += dot_last(carried[...], stationary[...])

    gradients(0, buffers[0])

    def two_steps(number, unused):
        gradients(2 * number + 1, buffers[1])
        contract(buffers[0], carried0)
        gradients(jnp.minimum(2 * number + 2, count - 1), buffers[0])
        contract(buffers[1], carried1)
        return unused

    lax.fori_loop(0, count // 2, two_steps, 0)
    if count % 2:
        contract(buffers[0], carried0)

    if packs:
        chunks = mode_count * mode_count // 128
        for chunk in range(chunks):
            part = conv_ref[chunk * 128 : (chunk + 1) * 128, :].T
            flat[pl.ds(chunk, mode_count, stride=chunks), :] = (
                part[:mode_count] + part[mode_count : 2 * mode_count]
            )
        devices, total, unused = message_ref.shape
        tail = fold(diss_ref[:, :mode_count])
        share = total - tail.shape[0]
        for device in range(devices):
            message_ref[device] = jnp.concatenate(
                [flat[device * share : (device + 1) * share, :], tail], axis=0
            ).astype(bf16)


def galerkin(core, sums, volume, sources, field_plan, halo_plan, rows_y, depth, message):
    height, lanes = sources[0].shape[1:]
    mode_count = height // 6
    used = sorted({e[0] for e in field_plan} | {o for e in halo_plan for o in e[:2]})
    number = {operand: place for place, operand in enumerate(used)}
    field_plan = tuple((number[operand], row) for operand, row in field_plan)
    halo_plan = tuple((number[p], number[q], row, cell) for p, q, row, cell in halo_plan)
    operands = list(sums or ()) + [volume] + [sources[operand] for operand in used]
    square = mode_count * mode_count
    scratch = []
    if message is None:
        out_shape = (
            jax.ShapeDtypeStruct((square, 128), f32),
            jax.ShapeDtypeStruct((mode_count, 128), f32),
        )
    else:
        out_shape = jax.ShapeDtypeStruct(message, bf16)
        scratch = [
            pltpu.VMEM((mode_count * square // 128, 128), f32),
            pltpu.VMEM((mode_count, 128), f32),
            pltpu.VMEM((square, 128), f32),
        ]
    buffers = [
        pltpu.VMEM((9 * mode_count, 2 * lanes), bf16),
        pltpu.VMEM((128, 18 * lanes), bf16),
        pltpu.VMEM((3 * mode_count, 2 * lanes), bf16),
        pltpu.VMEM((128, 6 * lanes), bf16),
    ]
    scratch += (
        buffers
        + buffers
        + [
            pltpu.VMEM((len(field_plan), height, lanes), bf16),
            pltpu.VMEM((len(halo_plan), height, lanes), bf16),
            pltpu.VMEM((len(halo_plan), height, lanes), bf16),
            pltpu.VMEM((depth, lanes), f32),
        ]
        + [pltpu.VMEM((square, 6 * lanes), bf16)] * (2 if lanes <= 128 else 1)
    )
    shapes = out_shape if message is None else (out_shape,)
    return pl.pallas_call(
        functools.partial(
            galerkin_kernel, field_plan, halo_plan, sums is not None, message is not None, rows_y,
            depth,
        ),
        in_specs=[smem] + [vmem] * len(operands),
        out_specs=vmem if message is not None else (vmem, vmem),
        out_shape=out_shape,
        scratch_shapes=scratch,
        compiler_params=room(*operands, *shapes, *scratch),
        cost_estimate=cost(1.4 * len(halo_plan) + 0.5),
        name="galerkin",
    )(core, *operands)


def finish_kernel(scales, moved_ref, conv_ref, diss_ref, total, rows_ref):
    total[...] = jnp.sum(moved_ref[...].astype(f32), axis=0)
    groups = conv_ref.shape[1] // 8
    for number, rows in enumerate(unpack(total, 0, groups)):
        rows_ref[pl.ds(number, groups, stride=8), :] = rows * scales[0]
    conv_ref[...] = rows_ref[...].T
    diss_ref[...] = unfold(total[3 * groups :, :], diss_ref.shape[0]) * scales[1]


def finish(moved, mode_count, scales):
    share = mode_count * mode_count // moved.shape[0]
    conv, diss = pl.pallas_call(
        functools.partial(finish_kernel, scales),
        in_specs=[vmem],
        out_specs=(vmem, vmem),
        out_shape=(
            jax.ShapeDtypeStruct((mode_count, share), f32),
            jax.ShapeDtypeStruct((mode_count, mode_count), f32),
        ),
        scratch_shapes=[
            pltpu.VMEM(moved.shape[1:], f32),
            pltpu.VMEM((share, mode_count), f32),
        ],
        compiler_params=room(moved, jax.ShapeDtypeStruct(moved.shape, f32)),
        name="finish",
    )(moved)
    return conv.T, diss


def per_device(modes, volume):
    local, comps, planes, rows_y, cells = modes.shape
    owners = lax.axis_size("mode")
    slabs = lax.axis_size("slab")
    devices = owners * slabs
    mode_count = local * owners
    lanes = planes * rows_y
    pairs = cells // 2 // owners
    me = lax.axis_index("mode").astype(jnp.int32).reshape(1)
    position = (lax.axis_index("slab") % 2).astype(jnp.int32).reshape(1)

    cuts = [0] + [int(pairs * cut) for cut in CUTS] + [pairs]
    chunks = len(cuts) - 1
    spans = tuple(
        (cuts[q] - (q == 0), cuts[q + 1] + (q == chunks - 1)) for q in range(chunks)
    )
    messages = head(me, modes, owners, spans)

    weights = pack(volume, messages[0][0], owners, planes)

    def exchange(blocks):
        moved = [blocks[0]]
        for shift in range(1, owners):
            moved.append(
                lax.ppermute(
                    blocks[shift], "mode", [(source, source ^ shift) for source in range(owners)]
                )
            )
        return moved

    inter = [(i, i + 1) for i in range(1, slabs - 1, 2)]
    inter += [(j, i) for i, j in inter]
    intra = [(i, i ^ 1) for i in range(slabs)]

    def after(value, *others):
        return lax.optimization_barrier((value, *others))[0]

    def place(row):
        if row < 0:
            return (1, 0)
        if row >= pairs:
            return (4 * chunks - 3, 0)
        q = max(q for q in range(chunks) if cuts[q] <= row)
        return (4 * q, row - cuts[q])

    share = mode_count**3 // devices
    fast = share % 384 == 0 and mode_count == 48
    message = (devices, share // 128 + mode_count // 4, 128) if fast else None

    def contraction(start, stop, sums, weights):
        last = stop == pairs
        field_plan = [place(row) for row in range(start - 1, stop + 1)]
        halo_plan = []
        for row in range(start, stop):
            operand, inner = place(row)
            halo_plan.append((operand + 2, operand + 3, inner, row))
        return galerkin(
            position, sums, weights, sources, field_plan, halo_plan, rows_y,
            cells // owners, message if last else None,
        )

    sources = []
    blocks = exchange(messages[0])
    for q in range(chunks):
        edge = 0 if q == 0 else (spans[q][1] - spans[q][0] - 1 if q == chunks - 1 else None)
        body, edge_row = assemble(me, blocks, edge)
        between = lax.ppermute(body, "slab", inter)
        within = lax.ppermute(body, "slab", intra)
        sources += [body, edge_row, between, within]
        if q == 0:
            weights = lax.all_to_all(after(weights, body), ("mode", "slab"), 0, 0, tiled=True)
        if q + 1 < chunks:
            blocks = exchange([after(message, *blocks[1:3]) for message in messages[q + 1]])

    sums = None
    done = 0
    for q in range(chunks):
        stop = pairs if q == chunks - 1 else cuts[q + 1] - 1
        sums = contraction(done, stop, sums, weights)
        done = stop

    total_cells = cells * rows_y * planes * slabs
    scales = (1.0 / math.sqrt(total_cells), viscosity / total_cells)
    if fast:
        moved = lax.all_to_all(sums, ("mode", "slab"), 0, 0, tiled=True)
        return finish(moved, mode_count, scales)
    conv, diss = sums
    conv = conv[:, :mode_count] + conv[:, mode_count : 2 * mode_count]
    padded = -(-share // 128) * 128
    conv = conv.T.reshape(devices, share)
    conv = jnp.pad(conv, ((0, 0), (0, padded - share))).reshape(devices, padded // 128, 128)
    extra = jnp.broadcast_to(
        diss[:, :mode_count].reshape(1, -1, 128), (devices, mode_count**2 // 128, 128)
    )
    packed = jnp.concatenate([conv, extra], axis=1).astype(bf16)
    moved = lax.all_to_all(packed, ("mode", "slab"), 0, 0, tiled=True).astype(f32).sum(0)
    convective = moved[: padded // 128].reshape(padded)[:share].reshape(-1, mode_count)
    dissipation = moved[padded // 128 :].reshape(mode_count, mode_count)
    return (convective * scales[0], dissipation * scales[1])


def solution(mesh):
    placed = (P("mode", None, "slab", None, None), P(None, ("mode", "slab"), None))
    return jax.shard_map(
        per_device,
        mesh=mesh,
        in_specs=placed,
        out_specs=(P(("mode", "slab"), None), P()),
        check_vma=False,
    )
```
